32 devices in a mesh: pole: 2 (over x), prow: 2 (over core), pcol: 8 (over z, y).
Axes of the slice: x: 2, y: 2, z: 4, core: 2. Of those that a mesh axis runs over, the one named last changes fastest.
Arguments:
- inverse_blocks: bfloat16 [16, 512, 4096], P('pole', 'prow', 'pcol'), parts along dimension 0, may hold values from -6 to 6
- lower: bfloat16 [32, 3, 512, 512], P('pole', None, ('prow', 'pcol')), parts along dimension 0, may hold values from -0.15625 to 0.15625
- diag_inverse: float32 [32, 512, 512], P('pole', ('prow', 'pcol')), parts along dimension 0, may hold values from -6 to 6
- structure: int32 [32, 3], P('pole'), parts along dimension 0, may hold values from 0 to 7, as said below
Outputs:
- diag_blocks: float32 [32, 512, 512], P('pole', ('prow', 'pcol')), parts along dimension 0
The draws below stay inside these ranges and needn't reach their ends.
There are 2 independent parts, one for each index of `pole`. The reference program is written for one: setup_inputs(seed, part) draws one part's arguments, and reference() takes and returns one part's arrays. A program takes and returns all parts, laid end to end along the dimension named above; each array names one. Nothing has to cross between parts.
Inputs may be any that keep to these rules, and one draw needn't show every extreme that they name: `structure`: each row names 3 different trailing supernodes; one trailing supernode is named by exactly 7 rows and none by more.
All inputs are finite; a program needn't handle non-finite values.
Results may differ from the reference program's by a relative error of at most 0.0021.
Values may be sent and summed in bfloat16 or wider, within the bound.
A program may use at most 128 MiB of HBM per device.

```python
import jax
import jax.numpy as jnp
from jax import lax

B = 512
S = 3
KS = 16
NT = 8
CAP = 7


def draw_structure(key, part):
    key = jax.random.fold_in(key, 11)
    key_order, key_roots, key_shift, key_shuffle = jax.random.split(key, 4)
    ordering = jax.random.permutation(key_order, NT).astype(jnp.int32)
    root_node = ordering[0]
    others = ordering[1:]
    offset = jax.random.randint(key_shift, (), 0, NT - 1)
    position = (jnp.arange(KS)[:, None] * S + jnp.arange(S)[None, :] + offset) % (NT - 1)
    listed = others[position]
    picked = jax.random.permutation(key_roots, KS)[:CAP]
    marked = jnp.zeros((KS,), jnp.int32).at[picked].set(1)
    first = jnp.where(marked == 1, root_node, listed[:, 0])
    listed = listed.at[:, 0].set(first)
    shuffles = jax.vmap(lambda single: jax.random.permutation(single, S))(jax.random.split(key_shuffle, KS))
    listed = jnp.take_along_axis(listed, shuffles, axis=1)
    return listed.astype(jnp.int32)


def block_scale(key, extent, cuts, low, largest):
    loudness, own = 1.0, jax.random.fold_in(key, 6)
    for axis_at, parts in cuts:
        draws = jnp.exp(jax.random.uniform(jax.random.fold_in(own, axis_at), (parts,), jnp.float32, low / len(cuts), largest / len(cuts)))
        loudness = loudness * jnp.repeat(draws, extent[axis_at] // parts).reshape([-1 if axis == axis_at else 1 for axis in range(len(extent))])
    return loudness


def bell_draw(rng, shape, width, most, cuts=(), kind=jnp.bfloat16):
    drawn = jax.random.normal(rng, shape, jnp.float32) * width
    if len(cuts) > 0:
        drawn = block_scale(rng, shape, cuts, -0.22, 0.18) * drawn
    return jnp.clip(drawn, min=-most, max=most).astype(kind)


def setup_inputs(seed: int = 0, part: int = 0) -> dict:
    splits = jax.random.split(jax.random.key(seed), 5)
    own_keys = jax.random.split(jax.random.fold_in(splits[4], part), 5)
    return {
        "inverse_blocks": bell_draw(own_keys[0], (NT, B, NT * B), 1.0, 6.0, ((1, 2), (2, 8))),
        "lower": bell_draw(own_keys[1], (KS, S, B, B), (S * B) ** -0.5, 0.15625, ((2, 16),)),
        "diag_inverse": bell_draw(own_keys[2], (KS, B, B), 1.0, 6.0, ((1, 16),), jnp.float32),
        "structure": draw_structure(jax.random.fold_in(jax.random.fold_in(splits[4], part), 71), part),
    }


def reference(inverse_blocks, lower, diag_inverse, structure):
    def per_node(node):
        block_rows = structure[node].astype(jnp.int32)
        factor = lower[node].astype(jnp.float32)
        total = jnp.zeros((B, B), jnp.float32)
        for t in range(S):
            column = lax.dynamic_slice_in_dim(inverse_blocks, (block_rows[t] * B).astype(jnp.int32), B, 2)
            chosen = column[block_rows].astype(jnp.float32)
            products = jnp.einsum("sab,bc->sac", chosen, factor[t]).astype(jnp.bfloat16)
            total = total + jnp.einsum("sba,sbc->ac", factor, products.astype(jnp.float32))
        return total

    coupling = lax.map(per_node, jnp.arange(KS, dtype=jnp.int32))
    return diag_inverse - coupling
```

```python
import functools

import jax
import jax.numpy as jnp
from jax import lax
from jax.experimental import pallas as pl
from jax.experimental.pallas import tpu as pltpu
from jax.sharding import PartitionSpec as P

B = 512


def per_device(inverse_blocks, lower, diag_inverse, structure):
    columns = lax.axis_size("pcol")
    own_column = lax.axis_index("pcol")
    node_count = structure.shape[0]
    slots_each = structure.shape[1]
    cap_slots = max(
        2, max(node_count // 4, (slots_each * node_count + columns - 2) // (columns - 1))
    )
    matches = structure[None, :, :] == jnp.arange(columns, dtype=jnp.int32)[:, None, None]
    present = jnp.any(matches, axis=2)
    position = jnp.cumsum(present.astype(jnp.int32), axis=1) - 1
    slot_match = present[:, :, None] & (
        position[:, :, None] == jnp.arange(cap_slots, dtype=jnp.int32)[None, None, :]
    )
    task_table = jnp.sum(
        slot_match.astype(jnp.int32) * jnp.arange(node_count, dtype=jnp.int32)[None, :, None],
        axis=1,
    )
    valid = jnp.any(slot_match, axis=1)
    my_tasks = lax.dynamic_index_in_dim(task_table, own_column, 0, False)
    my_valid = lax.dynamic_index_in_dim(valid, own_column, 0, False)
    flipped = jnp.swapaxes(lower, 0, 1)
    gathered = lax.all_gather(flipped, "pcol", axis=2, tiled=True)
    halves = gathered[:, my_tasks] * my_valid[None, :, None, None].astype(jnp.bfloat16)
    task_lists = structure[my_tasks]
    pick = (task_lists == own_column).astype(jnp.bfloat16)
    own_half = jnp.einsum("cs,scrb->crb", pick, halves, preferred_element_type=jnp.float32).astype(
        jnp.bfloat16
    )
    own_full = lax.all_gather(own_half, "prow", axis=1, tiled=True)
    contribs = []
    for index_slot in range(cap_slots):
        chosen = inverse_blocks[task_lists[index_slot]]
        products = jnp.einsum(
            "sab,bc->sac", chosen, own_full[index_slot], preferred_element_type=jnp.float32
        ).astype(jnp.bfloat16)
        contribs.append(
            jnp.einsum(
                "sba,sbc->ac", halves[:, index_slot], products, preferred_element_type=jnp.float32
            )
        )
    totals = jnp.zeros((node_count, B, B), jnp.float32)
    for index_slot in range(cap_slots):
        supernode = my_tasks[index_slot]
        current = lax.dynamic_index_in_dim(totals, supernode, 0, False)
        totals = lax.dynamic_update_index_in_dim(
            totals, current + contribs[index_slot], supernode, 0
        )
    coupling = lax.psum_scatter(totals, ("prow", "pcol"), scatter_dimension=1, tiled=True)
    return diag_inverse - coupling


MESH = pl.DeviceIdType.MESH


def fused_kernel(
    columns, cap, nodes, slots,
    tasks, own_slot, structure, places,
    inverse_ref, lower_ref, diag_ref,
    out_ref,
    picked, halves, full, partial, from_core, outgoing, incoming,
    pick_send, pick_recv, half_send, half_recv, core_send, core_recv, out_send, out_recv,
):
    pole = lax.axis_index("pole")
    core = lax.axis_index("prow")
    me = lax.axis_index("pcol")
    other = 1 - core
    peers = columns - 1

    barrier = pltpu.get_barrier_semaphore()

    def greet(step, carry):
        peer = lax.rem(me + 1 + step, columns)
        pl.semaphore_signal(barrier, inc=1, device_id=(pole, core, peer), device_id_type=MESH)
        return carry

    lax.fori_loop(0, peers, greet, 0)
    pl.semaphore_signal(barrier, inc=1, device_id=(pole, other, me), device_id_type=MESH)
    pl.semaphore_wait(barrier, columns)

    def pick_copy(index, step):
        peer = lax.rem(me + 1 + step, columns)
        return pltpu.make_async_remote_copy(
            src_ref=picked.at[index, step],
            dst_ref=halves.at[index, me],
            send_sem=pick_send.at[index, step],
            recv_sem=pick_recv.at[index, step],
            device_id=(pole, core, peer),
            device_id_type=MESH,
        )

    def half_copy(index):
        return pltpu.make_async_remote_copy(
            src_ref=full.at[index, core],
            dst_ref=full.at[index, core],
            send_sem=half_send.at[index],
            recv_sem=half_recv.at[index],
            device_id=(pole, other, me),
            device_id_type=MESH,
        )

    def core_copy(index):
        return pltpu.make_async_remote_copy(
            src_ref=partial.at[index, other],
            dst_ref=from_core.at[index],
            send_sem=core_send.at[index],
            recv_sem=core_recv.at[index],
            device_id=(pole, other, me),
            device_id_type=MESH,
        )

    def out_copy(index, step):
        peer = lax.rem(me + 1 + step, columns)
        return pltpu.make_async_remote_copy(
            src_ref=outgoing.at[index, peer],
            dst_ref=incoming.at[me, index],
            send_sem=out_send.at[index, step],
            recv_sem=out_recv.at[index, step],
            device_id=(pole, core, peer),
            device_id_type=MESH,
        )

    def send_task(index, carry):
        def to_peer(step, inner):
            peer = lax.rem(me + 1 + step, columns)
            picked[index, step] = lower_ref[tasks[peer * cap + index]]
            pick_copy(index, step).start()
            return inner

        lax.fori_loop(0, peers, to_peer, 0)
        halves[index, me] = lower_ref[tasks[me * cap + index]]
        return carry

    lax.fori_loop(0, cap, send_task, 0)

    def arrive(index):
        def one(step, inner):
            pick_copy(index, step).wait_recv()
            return inner

        lax.fori_loop(0, peers, one, 0)
        chosen_slot = own_slot[me * cap + index]
        mine = halves[index, :, 0]
        for slot in range(1, slots):
            mine = jnp.where(chosen_slot == slot, halves[index, :, slot], mine)
        full[index, core] = mine.reshape(full.shape[2:])
        half_copy(index).start()

    def multiply(index):
        half_copy(index).wait_recv()
        node = tasks[me * cap + index]
        factor = full[index].reshape(B, B)
        total = jnp.zeros((B, B), jnp.float32)
        for slot in range(slots):
            chosen = inverse_ref[structure[node * slots + slot]]
            products = jnp.dot(chosen, factor, preferred_element_type=jnp.float32).astype(
                jnp.bfloat16
            )
            rows = halves[index, :, slot].reshape(B // 2, B)
            total = total + lax.dot_general(
                rows, products, (((0,), (0,)), ((), ())), preferred_element_type=jnp.float32
            )
        partial[index] = total.reshape(partial.shape[1:])
        core_copy(index).start()

    def hand_out(index):
        core_copy(index).wait_recv()
        summed = (partial[index, core] + from_core[index]).astype(jnp.bfloat16)
        outgoing[index] = summed.reshape(outgoing.shape[1:])
        incoming[me, index] = outgoing[index, me]

        def one(step, inner):
            out_copy(index, step).start()
            return inner

        lax.fori_loop(0, peers, one, 0)

    def step_all(step, carry):
        @pl.when(step < cap)
        def _():
            arrive(step)

        @pl.when((step >= 1) & (step < cap + 1))
        def _():
            multiply(step - 1)

        @pl.when(step >= 2)
        def _():
            hand_out(step - 2)

        return carry

    lax.fori_loop(0, cap + 2, step_all, 0)

    def landed(index, carry):
        def one(step, inner):
            out_copy(index, step).wait_recv()
            return inner

        lax.fori_loop(0, peers, one, 0)
        return carry

    lax.fori_loop(0, cap, landed, 0)

    def finish(node, carry):
        value = jnp.zeros(out_ref.shape[1:], jnp.float32)
        for slot in range(slots):
            place = node * slots + slot
            value = value + incoming[structure[place], places[place]].astype(jnp.float32)
        out_ref[node] = diag_ref[node] - value
        return carry

    lax.fori_loop(0, nodes, finish, 0)

    def sent(index, carry):
        def one(step, inner):
            pick_copy(index, step).wait_send()
            out_copy(index, step).wait_send()
            return inner

        lax.fori_loop(0, peers, one, 0)
        half_copy(index).wait_send()
        core_copy(index).wait_send()
        return carry

    lax.fori_loop(0, cap, sent, 0)


def per_device_fused(inverse_blocks, lower, diag_inverse, structure):
    columns = lax.axis_size("pcol")
    nodes, slots = structure.shape
    chunk = lower.shape[2]
    cap = max(2, max(nodes // 4, (slots * nodes + columns - 2) // (columns - 1)))
    node_ids = jnp.arange(nodes, dtype=jnp.int32)
    matches = structure[None] == jnp.arange(columns, dtype=jnp.int32)[:, None, None]
    present = jnp.any(matches, axis=2)
    earlier = node_ids[None, :] < node_ids[:, None]
    position = jnp.sum((present[:, None, :] & earlier[None]).astype(jnp.int32), axis=2)
    hit = present[:, None, :] & (
        position[:, None, :] == jnp.arange(cap, dtype=jnp.int32)[None, :, None]
    )
    tasks = jnp.sum(jnp.where(hit, node_ids[None, None, :], 0), axis=2)
    slot_of = jnp.sum(
        jnp.where(matches, jnp.arange(slots, dtype=jnp.int32)[None, None, :], 0), axis=2
    )
    own_slot = jnp.sum(jnp.where(hit, slot_of[:, None, :], 0), axis=2)
    places = jnp.sum(jnp.where(matches, position[:, :, None], 0), axis=0)
    smem = pl.BlockSpec(memory_space=pltpu.SMEM)
    vmem = pl.BlockSpec(memory_space=pltpu.VMEM)
    peers = columns - 1
    dma = pltpu.SemaphoreType.DMA
    return pl.pallas_call(
        functools.partial(fused_kernel, columns, cap, nodes, slots),
        out_shape=jax.ShapeDtypeStruct(diag_inverse.shape, jnp.float32),
        in_specs=[smem] * 4 + [vmem] * 3,
        out_specs=vmem,
        scratch_shapes=[
            pltpu.VMEM((cap, peers, slots, chunk, B), jnp.bfloat16),
            pltpu.VMEM((cap, columns, slots, chunk, B), jnp.bfloat16),
            pltpu.VMEM((cap, 2, B // 2, B), jnp.bfloat16),
            pltpu.VMEM((cap, 2, B // 2, B), jnp.float32),
            pltpu.VMEM((cap, B // 2, B), jnp.float32),
            pltpu.VMEM((cap, columns, chunk, B), jnp.bfloat16),
            pltpu.VMEM((columns, cap, chunk, B), jnp.bfloat16),
            dma((cap, peers)),
            dma((cap, peers)),
            dma((cap,)),
            dma((cap,)),
            dma((cap,)),
            dma((cap,)),
            dma((cap, peers)),
            dma((cap, peers)),
        ],
        compiler_params=pltpu.CompilerParams(
            collective_id=0, has_side_effects=True, vmem_limit_bytes=48 * 1024 * 1024
        ),
    )(
        tasks.reshape(-1), own_slot.reshape(-1), structure.reshape(-1), places.reshape(-1),
        inverse_blocks, lower, diag_inverse,
    )


def solution(mesh):
    placed = (
        P("pole", "prow", "pcol"),
        P("pole", None, ("prow", "pcol"), None),
        P("pole", ("prow", "pcol"), None),
        P("pole", None),
    )
    body = per_device
    whole_tiles = B % (16 * mesh.shape["prow"] * mesh.shape["pcol"]) == 0
    if mesh.shape["prow"] == 2 and mesh.shape["pcol"] == 8 and whole_tiles:
        body = per_device_fused
    return jax.shard_map(
        body,
        mesh=mesh,
        in_specs=placed,
        out_specs=P("pole", ("prow", "pcol"), None),
        check_vma=False,
    )
```

```python
import functools

import jax
import jax.numpy as jnp
from jax import lax
from jax.experimental import pallas as pl
from jax.experimental.pallas import tpu as pltpu
from jax.sharding import PartitionSpec as P

B = 512


def per_device(inverse_blocks, lower, diag_inverse, structure):
    columns = lax.axis_size("pcol")
    own_column = lax.axis_index("pcol")
    node_count = structure.shape[0]
    slots_each = structure.shape[1]
    cap_slots = max(
        2, max(node_count // 4, (slots_each * node_count + columns - 2) // (columns - 1))
    )
    matches = structure[None, :, :] == jnp.arange(columns, dtype=jnp.int32)[:, None, None]
    present = jnp.any(matches, axis=2)
    position = jnp.cumsum(present.astype(jnp.int32), axis=1) - 1
    slot_match = present[:, :, None] & (
        position[:, :, None] == jnp.arange(cap_slots, dtype=jnp.int32)[None, None, :]
    )
    task_table = jnp.sum(
        slot_match.astype(jnp.int32) * jnp.arange(node_count, dtype=jnp.int32)[None, :, None],
        axis=1,
    )
    valid = jnp.any(slot_match, axis=1)
    my_tasks = lax.dynamic_index_in_dim(task_table, own_column, 0, False)
    my_valid = lax.dynamic_index_in_dim(valid, own_column, 0, False)
    flipped = jnp.swapaxes(lower, 0, 1)
    gathered = lax.all_gather(flipped, "pcol", axis=2, tiled=True)
    halves = gathered[:, my_tasks] * my_valid[None, :, None, None].astype(jnp.bfloat16)
    task_lists = structure[my_tasks]
    pick = (task_lists == own_column).astype(jnp.bfloat16)
    own_half = jnp.einsum("cs,scrb->crb", pick, halves, preferred_element_type=jnp.float32).astype(
        jnp.bfloat16
    )
    own_full = lax.all_gather(own_half, "prow", axis=1, tiled=True)
    contribs = []
    for index_slot in range(cap_slots):
        chosen = inverse_blocks[task_lists[index_slot]]
        products = jnp.einsum(
            "sab,bc->sac", chosen, own_full[index_slot], preferred_element_type=jnp.float32
        ).astype(jnp.bfloat16)
        contribs.append(
            jnp.einsum(
                "sba,sbc->ac", halves[:, index_slot], products, preferred_element_type=jnp.float32
            )
        )
    totals = jnp.zeros((node_count, B, B), jnp.float32)
    for index_slot in range(cap_slots):
        supernode = my_tasks[index_slot]
        current = lax.dynamic_index_in_dim(totals, supernode, 0, False)
        totals = lax.dynamic_update_index_in_dim(
            totals, current + contribs[index_slot], supernode, 0
        )
    coupling = lax.psum_scatter(totals, ("prow", "pcol"), scatter_dimension=1, tiled=True)
    return diag_inverse - coupling


MESH = pl.DeviceIdType.MESH


def fused_kernel(
    columns, cap, nodes, slots,
    tasks, own_slot, structure, places,
    inverse_hbm, lower_ref, diag_hbm,
    out_ref,
    inverse_ref, diag_ref, mirrored, picked, halves, full, partial, from_core, outgoing, incoming,
    load_sem, mirror_send, mirror_recv, pick_send, pick_recv, half_send, half_recv, core_send, core_recv, out_send, out_recv,
):
    pole = lax.axis_index("pole")
    core = lax.axis_index("prow")
    me = lax.axis_index("pcol")
    other = 1 - core
    peers = columns - 1
    mates = columns // 2 - 1
    base = (me // (mates + 1)) * (mates + 1)
    mirror = columns - 2 - me + 2 * (me % 2)
    parts = mirror_send.shape[0]
    span = nodes // parts

    load_inverse = pltpu.make_async_copy(inverse_hbm, inverse_ref, load_sem.at[0])
    load_diag = pltpu.make_async_copy(diag_hbm, diag_ref, load_sem.at[1])

    barrier = pltpu.get_barrier_semaphore()

    def greet(step, carry):
        peer = lax.rem(me + 1 + step, columns)
        pl.semaphore_signal(barrier, inc=1, device_id=(pole, core, peer), device_id_type=MESH)
        return carry

    lax.fori_loop(0, peers, greet, 0)
    pl.semaphore_signal(barrier, inc=1, device_id=(pole, other, me), device_id_type=MESH)
    pl.semaphore_wait(barrier, columns)

    def mate(step):
        return base + lax.rem(me - base + 1 + step, mates + 1)

    def mirror_copy(part):
        piece = pl.ds(part * span, span)
        return pltpu.make_async_remote_copy(
            src_ref=lower_ref.at[piece],
            dst_ref=mirrored.at[piece],
            send_sem=mirror_send.at[part],
            recv_sem=mirror_recv.at[part],
            device_id=(pole, core, mirror),
            device_id_type=MESH,
        )

    def pick_copy(relayed, index, step):
        return pltpu.make_async_remote_copy(
            src_ref=picked.at[relayed, index, step],
            dst_ref=halves.at[index, mirror if relayed else me],
            send_sem=pick_send.at[relayed, index, step],
            recv_sem=pick_recv.at[relayed, index, step],
            device_id=(pole, core, mate(step)),
            device_id_type=MESH,
        )

    def half_copy(index):
        return pltpu.make_async_remote_copy(
            src_ref=full.at[index, core],
            dst_ref=full.at[index, core],
            send_sem=half_send.at[index],
            recv_sem=half_recv.at[index],
            device_id=(pole, other, me),
            device_id_type=MESH,
        )

    def core_copy(index):
        return pltpu.make_async_remote_copy(
            src_ref=partial.at[index, other],
            dst_ref=from_core.at[index],
            send_sem=core_send.at[index],
            recv_sem=core_recv.at[index],
            device_id=(pole, other, me),
            device_id_type=MESH,
        )

    def out_copy(index, step):
        peer = lax.rem(me + 1 + step, columns)
        return pltpu.make_async_remote_copy(
            src_ref=outgoing.at[index, peer],
            dst_ref=incoming.at[me, index],
            send_sem=out_send.at[index, step],
            recv_sem=out_recv.at[index, step],
            device_id=(pole, core, peer),
            device_id_type=MESH,
        )

    def send_tasks(relayed, source):
        def send_task(index, carry):
            def to_mate(step, inner):
                picked[relayed, index, step] = source[tasks[mate(step) * cap + index]]
                pick_copy(relayed, index, step).start()
                return inner

            lax.fori_loop(0, mates, to_mate, 0)
            halves[index, mirror if relayed else me] = source[tasks[me * cap + index]]
            return carry

        lax.fori_loop(0, cap, send_task, 0)

    for part in range(parts):
        mirror_copy(part).start()
    load_inverse.start()
    load_diag.start()
    send_tasks(0, lower_ref)
    for part in range(parts):
        mirror_copy(part).wait_recv()
    send_tasks(1, mirrored)
    load_inverse.wait()
    load_diag.wait()

    def arrive(index):
        def one(step, inner):
            pick_copy(0, index, step).wait_recv()
            pick_copy(1, index, step).wait_recv()
            return inner

        lax.fori_loop(0, mates, one, 0)
        chosen_slot = own_slot[me * cap + index]
        mine = halves[index, :, 0]
        for slot in range(1, slots):
            mine = jnp.where(chosen_slot == slot, halves[index, :, slot], mine)
        full[index, core] = mine.reshape(full.shape[2:])
        half_copy(index).start()

    def multiply(index):
        half_copy(index).wait_recv()
        node = tasks[me * cap + index]
        factor = full[index].reshape(B, B)
        total = jnp.zeros((B, B), jnp.float32)
        for slot in range(slots):
            chosen = inverse_ref[structure[node * slots + slot]]
            products = jnp.dot(chosen, factor, preferred_element_type=jnp.float32).astype(
                jnp.bfloat16
            )
            rows = halves[index, :, slot].reshape(B // 2, B)
            total = total + lax.dot_general(
                rows, products, (((0,), (0,)), ((), ())), preferred_element_type=jnp.float32
            )
        partial[index] = total.reshape(partial.shape[1:])
        core_copy(index).start()

    def hand_out(index):
        core_copy(index).wait_recv()
        summed = (partial[index, core] + from_core[index]).astype(jnp.bfloat16)
        outgoing[index] = summed.reshape(outgoing.shape[1:])
        incoming[me, index] = outgoing[index, me]

        def one(step, inner):
            out_copy(index, step).start()
            return inner

        lax.fori_loop(0, peers, one, 0)

    def step_all(step, carry):
        @pl.when(step < cap)
        def _():
            arrive(step)

        @pl.when((step >= 1) & (step < cap + 1))
        def _():
            multiply(step - 1)

        @pl.when(step >= 2)
        def _():
            hand_out(step - 2)

        return carry

    lax.fori_loop(0, cap + 2, step_all, 0)

    def landed(index, carry):
        def one(step, inner):
            out_copy(index, step).wait_recv()
            return inner

        lax.fori_loop(0, peers, one, 0)
        return carry

    lax.fori_loop(0, cap, landed, 0)

    def finish(node, carry):
        value = jnp.zeros(out_ref.shape[1:], jnp.float32)
        for slot in range(slots):
            place = node * slots + slot
            value = value + incoming[structure[place], places[place]].astype(jnp.float32)
        out_ref[node] = diag_ref[node] - value
        return carry

    lax.fori_loop(0, nodes, finish, 0)

    def sent(index, carry):
        def one_pick(step, inner):
            pick_copy(0, index, step).wait_send()
            pick_copy(1, index, step).wait_send()
            return inner

        def one_out(step, inner):
            out_copy(index, step).wait_send()
            return inner

        lax.fori_loop(0, mates, one_pick, 0)
        lax.fori_loop(0, peers, one_out, 0)
        half_copy(index).wait_send()
        core_copy(index).wait_send()
        return carry

    lax.fori_loop(0, cap, sent, 0)
    for part in range(parts):
        mirror_copy(part).wait_send()


def per_device_fused(inverse_blocks, lower, diag_inverse, structure):
    columns = lax.axis_size("pcol")
    nodes, slots = structure.shape
    chunk = lower.shape[2]
    cap = max(2, max(nodes // 4, (slots * nodes + columns - 2) // (columns - 1)))
    node_ids = jnp.arange(nodes, dtype=jnp.int32)
    matches = structure[None] == jnp.arange(columns, dtype=jnp.int32)[:, None, None]
    present = jnp.any(matches, axis=2)
    earlier = node_ids[None, :] < node_ids[:, None]
    position = jnp.sum((present[:, None, :] & earlier[None]).astype(jnp.int32), axis=2)
    hit = present[:, None, :] & (
        position[:, None, :] == jnp.arange(cap, dtype=jnp.int32)[None, :, None]
    )
    tasks = jnp.sum(jnp.where(hit, node_ids[None, None, :], 0), axis=2)
    slot_of = jnp.sum(
        jnp.where(matches, jnp.arange(slots, dtype=jnp.int32)[None, None, :], 0), axis=2
    )
    own_slot = jnp.sum(jnp.where(hit, slot_of[:, None, :], 0), axis=2)
    places = jnp.sum(jnp.where(matches, position[:, :, None], 0), axis=0)
    smem = pl.BlockSpec(memory_space=pltpu.SMEM)
    vmem = pl.BlockSpec(memory_space=pltpu.VMEM)
    anywhere = pl.BlockSpec(memory_space=pl.ANY)
    peers = columns - 1
    mates = columns // 2 - 1
    parts = 4 if nodes % 4 == 0 else 1
    dma = pltpu.SemaphoreType.DMA
    return pl.pallas_call(
        functools.partial(fused_kernel, columns, cap, nodes, slots),
        out_shape=jax.ShapeDtypeStruct(diag_inverse.shape, jnp.float32),
        in_specs=[smem] * 4 + [anywhere, vmem, anywhere],
        out_specs=vmem,
        scratch_shapes=[
            pltpu.VMEM(inverse_blocks.shape, jnp.bfloat16),
            pltpu.VMEM(diag_inverse.shape, jnp.float32),
            pltpu.VMEM(lower.shape, jnp.bfloat16),
            pltpu.VMEM((2, cap, mates, slots, chunk, B), jnp.bfloat16),
            pltpu.VMEM((cap, columns, slots, chunk, B), jnp.bfloat16),
            pltpu.VMEM((cap, 2, B // 2, B), jnp.bfloat16),
            pltpu.VMEM((cap, 2, B // 2, B), jnp.float32),
            pltpu.VMEM((cap, B // 2, B), jnp.float32),
            pltpu.VMEM((cap, columns, chunk, B), jnp.bfloat16),
            pltpu.VMEM((columns, cap, chunk, B), jnp.bfloat16),
            dma((2,)),
            dma((parts,)),
            dma((parts,)),
            dma((2, cap, mates)),
            dma((2, cap, mates)),
            dma((cap,)),
            dma((cap,)),
            dma((cap,)),
            dma((cap,)),
            dma((cap, peers)),
            dma((cap, peers)),
        ],
        compiler_params=pltpu.CompilerParams(
            collective_id=0, has_side_effects=True, vmem_limit_bytes=48 * 1024 * 1024
        ),
    )(
        tasks.reshape(-1), own_slot.reshape(-1), structure.reshape(-1), places.reshape(-1),
        inverse_blocks, lower, diag_inverse,
    )


def solution(mesh):
    placed = (
        P("pole", "prow", "pcol"),
        P("pole", None, ("prow", "pcol"), None),
        P("pole", ("prow", "pcol"), None),
        P("pole", None),
    )
    body = per_device
    whole_tiles = B % (16 * mesh.shape["prow"] * mesh.shape["pcol"]) == 0
    if mesh.shape["prow"] == 2 and mesh.shape["pcol"] == 8 and whole_tiles:
        body = per_device_fused
    return jax.shard_map(
        body,
        mesh=mesh,
        in_specs=placed,
        out_specs=P("pole", ("prow", "pcol"), None),
        check_vma=False,
    )
```

```python
import functools

import jax
import jax.numpy as jnp
from jax import lax
from jax.experimental import pallas as pl
from jax.experimental.pallas import tpu as pltpu
from jax.sharding import PartitionSpec as P

B = 512


def per_device(inverse_blocks, lower, diag_inverse, structure):
    columns = lax.axis_size("pcol")
    own_column = lax.axis_index("pcol")
    node_count = structure.shape[0]
    slots_each = structure.shape[1]
    cap_slots = max(
        2, max(node_count // 4, (slots_each * node_count + columns - 2) // (columns - 1))
    )
    matches = structure[None, :, :] == jnp.arange(columns, dtype=jnp.int32)[:, None, None]
    present = jnp.any(matches, axis=2)
    position = jnp.cumsum(present.astype(jnp.int32), axis=1) - 1
    slot_match = present[:, :, None] & (
        position[:, :, None] == jnp.arange(cap_slots, dtype=jnp.int32)[None, None, :]
    )
    task_table = jnp.sum(
        slot_match.astype(jnp.int32) * jnp.arange(node_count, dtype=jnp.int32)[None, :, None],
        axis=1,
    )
    valid = jnp.any(slot_match, axis=1)
    my_tasks = lax.dynamic_index_in_dim(task_table, own_column, 0, False)
    my_valid = lax.dynamic_index_in_dim(valid, own_column, 0, False)
    flipped = jnp.swapaxes(lower, 0, 1)
    gathered = lax.all_gather(flipped, "pcol", axis=2, tiled=True)
    halves = gathered[:, my_tasks] * my_valid[None, :, None, None].astype(jnp.bfloat16)
    task_lists = structure[my_tasks]
    pick = (task_lists == own_column).astype(jnp.bfloat16)
    own_half = jnp.einsum("cs,scrb->crb", pick, halves, preferred_element_type=jnp.float32).astype(
        jnp.bfloat16
    )
    own_full = lax.all_gather(own_half, "prow", axis=1, tiled=True)
    contribs = []
    for index_slot in range(cap_slots):
        chosen = inverse_blocks[task_lists[index_slot]]
        products = jnp.einsum(
            "sab,bc->sac", chosen, own_full[index_slot], preferred_element_type=jnp.float32
        ).astype(jnp.bfloat16)
        contribs.append(
            jnp.einsum(
                "sba,sbc->ac", halves[:, index_slot], products, preferred_element_type=jnp.float32
            )
        )
    totals = jnp.zeros((node_count, B, B), jnp.float32)
    for index_slot in range(cap_slots):
        supernode = my_tasks[index_slot]
        current = lax.dynamic_index_in_dim(totals, supernode, 0, False)
        totals = lax.dynamic_update_index_in_dim(
            totals, current + contribs[index_slot], supernode, 0
        )
    coupling = lax.psum_scatter(totals, ("prow", "pcol"), scatter_dimension=1, tiled=True)
    return diag_inverse - coupling


MESH = pl.DeviceIdType.MESH


def fused_kernel(
    columns, cap, nodes, slots,
    tasks, own_slot, structure, places,
    inverse_hbm, lower_ref, diag_hbm,
    out_ref,
    inverse_ref, diag_ref, mirrored, picked, halves, full, partial, from_core, outgoing, incoming,
    load_sem, mirror_send, mirror_recv, pick_send, pick_recv, half_send, half_recv, core_send, core_recv, out_send, out_recv,
):
    pole = lax.axis_index("pole")
    core = lax.axis_index("prow")
    me = lax.axis_index("pcol")
    other = 1 - core
    peers = columns - 1
    mates = columns // 2 - 1
    ahead = min(2, cap)
    base = (me // (mates + 1)) * (mates + 1)
    mirror = columns - 2 - me + 2 * (me % 2)
    parts = mirror_send.shape[0]
    span = nodes // parts

    load_inverse = pltpu.make_async_copy(inverse_hbm, inverse_ref, load_sem.at[0])
    load_diag = pltpu.make_async_copy(diag_hbm, diag_ref, load_sem.at[1])

    barrier = pltpu.get_barrier_semaphore()

    def greet(step, carry):
        peer = lax.rem(me + 1 + step, columns)
        pl.semaphore_signal(barrier, inc=1, device_id=(pole, core, peer), device_id_type=MESH)
        return carry

    lax.fori_loop(0, peers, greet, 0)
    pl.semaphore_signal(barrier, inc=1, device_id=(pole, other, me), device_id_type=MESH)
    pl.semaphore_wait(barrier, columns)

    def mate(step):
        return base + lax.rem(me - base + 1 + step, mates + 1)

    def mirror_copy(part):
        piece = pl.ds(part * span, span)
        return pltpu.make_async_remote_copy(
            src_ref=lower_ref.at[piece],
            dst_ref=mirrored.at[piece],
            send_sem=mirror_send.at[part],
            recv_sem=mirror_recv.at[part],
            device_id=(pole, core, mirror),
            device_id_type=MESH,
        )

    def pick_copy(relayed, index, step):
        return pltpu.make_async_remote_copy(
            src_ref=picked.at[relayed, index, step],
            dst_ref=halves.at[index, mirror if relayed else me],
            send_sem=pick_send.at[relayed, index, step],
            recv_sem=pick_recv.at[relayed, index, step],
            device_id=(pole, core, mate(step)),
            device_id_type=MESH,
        )

    def half_copy(index):
        return pltpu.make_async_remote_copy(
            src_ref=full.at[index, core],
            dst_ref=full.at[index, core],
            send_sem=half_send.at[index],
            recv_sem=half_recv.at[index],
            device_id=(pole, other, me),
            device_id_type=MESH,
        )

    def core_copy(index):
        return pltpu.make_async_remote_copy(
            src_ref=partial.at[index, other],
            dst_ref=from_core.at[index],
            send_sem=core_send.at[index],
            recv_sem=core_recv.at[index],
            device_id=(pole, other, me),
            device_id_type=MESH,
        )

    def out_copy(index, step):
        peer = lax.rem(me + 1 + step, columns)
        return pltpu.make_async_remote_copy(
            src_ref=outgoing.at[index, peer],
            dst_ref=incoming.at[me, index],
            send_sem=out_send.at[index, step],
            recv_sem=out_recv.at[index, step],
            device_id=(pole, core, peer),
            device_id_type=MESH,
        )

    def send_task(relayed, source, index):
        def to_mate(step, inner):
            picked[relayed, index, step] = source[tasks[mate(step) * cap + index]]
            pick_copy(relayed, index, step).start()
            return inner

        lax.fori_loop(0, mates, to_mate, 0)
        halves[index, mirror if relayed else me] = source[tasks[me * cap + index]]

    def send_own(index, carry):
        send_task(0, lower_ref, index)
        return carry

    for part in range(parts):
        mirror_copy(part).start()
    load_inverse.start()
    load_diag.start()
    lax.fori_loop(0, cap, send_own, 0)
    for part in range(parts):
        mirror_copy(part).wait_recv()
    for index in range(ahead):
        send_task(1, mirrored, index)
    load_inverse.wait()
    load_diag.wait()

    def arrive(index):
        def one(step, inner):
            pick_copy(0, index, step).wait_recv()
            pick_copy(1, index, step).wait_recv()
            return inner

        lax.fori_loop(0, mates, one, 0)
        chosen_slot = own_slot[me * cap + index]
        mine = halves[index, :, 0]
        for slot in range(1, slots):
            mine = jnp.where(chosen_slot == slot, halves[index, :, slot], mine)
        full[index, core] = mine.reshape(full.shape[2:])
        half_copy(index).start()

    def multiply(index):
        half_copy(index).wait_recv()
        node = tasks[me * cap + index]
        factor = full[index].reshape(B, B)
        total = jnp.zeros((B, B), jnp.float32)
        for slot in range(slots):
            chosen = inverse_ref[structure[node * slots + slot]]
            products = jnp.dot(chosen, factor, preferred_element_type=jnp.float32).astype(
                jnp.bfloat16
            )
            rows = halves[index, :, slot].reshape(B // 2, B)
            total = total + lax.dot_general(
                rows, products, (((0,), (0,)), ((), ())), preferred_element_type=jnp.float32
            )
        partial[index] = total.reshape(partial.shape[1:])
        core_copy(index).start()

    def hand_out(index):
        core_copy(index).wait_recv()
        summed = (partial[index, core] + from_core[index]).astype(jnp.bfloat16)
        outgoing[index] = summed.reshape(outgoing.shape[1:])
        incoming[me, index] = outgoing[index, me]

        def one(step, inner):
            out_copy(index, step).start()
            return inner

        lax.fori_loop(0, peers, one, 0)

    def step_all(step, carry):
        @pl.when(step < cap)
        def _():
            arrive(step)

        @pl.when(step < cap - ahead)
        def _():
            send_task(1, mirrored, step + ahead)

        @pl.when((step >= 1) & (step < cap + 1))
        def _():
            multiply(step - 1)

        @pl.when(step >= 2)
        def _():
            hand_out(step - 2)

        return carry

    lax.fori_loop(0, cap + 2, step_all, 0)

    def landed(index, carry):
        def one(step, inner):
            out_copy(index, step).wait_recv()
            return inner

        lax.fori_loop(0, peers, one, 0)
        return carry

    lax.fori_loop(0, cap, landed, 0)

    def finish(node, carry):
        value = jnp.zeros(out_ref.shape[1:], jnp.float32)
        for slot in range(slots):
            place = node * slots + slot
            value = value + incoming[structure[place], places[place]].astype(jnp.float32)
        out_ref[node] = diag_ref[node] - value
        return carry

    lax.fori_loop(0, nodes, finish, 0)

    def sent(index, carry):
        def one_pick(step, inner):
            pick_copy(0, index, step).wait_send()
            pick_copy(1, index, step).wait_send()
            return inner

        def one_out(step, inner):
            out_copy(index, step).wait_send()
            return inner

        lax.fori_loop(0, mates, one_pick, 0)
        lax.fori_loop(0, peers, one_out, 0)
        half_copy(index).wait_send()
        core_copy(index).wait_send()
        return carry

    lax.fori_loop(0, cap, sent, 0)
    for part in range(parts):
        mirror_copy(part).wait_send()


def per_device_fused(inverse_blocks, lower, diag_inverse, structure):
    columns = lax.axis_size("pcol")
    nodes, slots = structure.shape
    chunk = lower.shape[2]
    cap = max(2, max(nodes // 4, (slots * nodes + columns - 2) // (columns - 1)))
    node_ids = jnp.arange(nodes, dtype=jnp.int32)
    matches = structure[None] == jnp.arange(columns, dtype=jnp.int32)[:, None, None]
    present = jnp.any(matches, axis=2)
    earlier = node_ids[None, :] < node_ids[:, None]
    position = jnp.sum((present[:, None, :] & earlier[None]).astype(jnp.int32), axis=2)
    hit = present[:, None, :] & (
        position[:, None, :] == jnp.arange(cap, dtype=jnp.int32)[None, :, None]
    )
    tasks = jnp.sum(jnp.where(hit, node_ids[None, None, :], 0), axis=2)
    slot_of = jnp.sum(
        jnp.where(matches, jnp.arange(slots, dtype=jnp.int32)[None, None, :], 0), axis=2
    )
    own_slot = jnp.sum(jnp.where(hit, slot_of[:, None, :], 0), axis=2)
    places = jnp.sum(jnp.where(matches, position[:, :, None], 0), axis=0)
    smem = pl.BlockSpec(memory_space=pltpu.SMEM)
    vmem = pl.BlockSpec(memory_space=pltpu.VMEM)
    anywhere = pl.BlockSpec(memory_space=pl.ANY)
    peers = columns - 1
    mates = columns // 2 - 1
    parts = 4 if nodes % 4 == 0 else 1
    dma = pltpu.SemaphoreType.DMA
    return pl.pallas_call(
        functools.partial(fused_kernel, columns, cap, nodes, slots),
        out_shape=jax.ShapeDtypeStruct(diag_inverse.shape, jnp.float32),
        in_specs=[smem] * 4 + [anywhere, vmem, anywhere],
        out_specs=vmem,
        scratch_shapes=[
            pltpu.VMEM(inverse_blocks.shape, jnp.bfloat16),
            pltpu.VMEM(diag_inverse.shape, jnp.float32),
            pltpu.VMEM(lower.shape, jnp.bfloat16),
            pltpu.VMEM((2, cap, mates, slots, chunk, B), jnp.bfloat16),
            pltpu.VMEM((cap, columns, slots, chunk, B), jnp.bfloat16),
            pltpu.VMEM((cap, 2, B // 2, B), jnp.bfloat16),
            pltpu.VMEM((cap, 2, B // 2, B), jnp.float32),
            pltpu.VMEM((cap, B // 2, B), jnp.float32),
            pltpu.VMEM((cap, columns, chunk, B), jnp.bfloat16),
            pltpu.VMEM((columns, cap, chunk, B), jnp.bfloat16),
            dma((2,)),
            dma((parts,)),
            dma((parts,)),
            dma((2, cap, mates)),
            dma((2, cap, mates)),
            dma((cap,)),
            dma((cap,)),
            dma((cap,)),
            dma((cap,)),
            dma((cap, peers)),
            dma((cap, peers)),
        ],
        compiler_params=pltpu.CompilerParams(
            collective_id=0, has_side_effects=True, vmem_limit_bytes=48 * 1024 * 1024
        ),
    )(
        tasks.reshape(-1), own_slot.reshape(-1), structure.reshape(-1), places.reshape(-1),
        inverse_blocks, lower, diag_inverse,
    )


def solution(mesh):
    placed = (
        P("pole", "prow", "pcol"),
        P("pole", None, ("prow", "pcol"), None),
        P("pole", ("prow", "pcol"), None),
        P("pole", None),
    )
    body = per_device
    whole_tiles = B % (16 * mesh.shape["prow"] * mesh.shape["pcol"]) == 0
    if mesh.shape["prow"] == 2 and mesh.shape["pcol"] == 8 and whole_tiles:
        body = per_device_fused
    return jax.shard_map(
        body,
        mesh=mesh,
        in_specs=placed,
        out_specs=P("pole", ("prow", "pcol"), None),
        check_vma=False,
    )
```

```python
import functools

import jax
import jax.numpy as jnp
from jax import lax
from jax.experimental import pallas as pl
from jax.experimental.pallas import tpu as pltpu
from jax.sharding import PartitionSpec as P

B = 512


def per_device(inverse_blocks, lower, diag_inverse, structure):
    columns = lax.axis_size("pcol")
    own_column = lax.axis_index("pcol")
    node_count = structure.shape[0]
    slots_each = structure.shape[1]
    cap_slots = max(
        2, max(node_count // 4, (slots_each * node_count + columns - 2) // (columns - 1))
    )
    matches = structure[None, :, :] == jnp.arange(columns, dtype=jnp.int32)[:, None, None]
    present = jnp.any(matches, axis=2)
    position = jnp.cumsum(present.astype(jnp.int32), axis=1) - 1
    slot_match = present[:, :, None] & (
        position[:, :, None] == jnp.arange(cap_slots, dtype=jnp.int32)[None, None, :]
    )
    task_table = jnp.sum(
        slot_match.astype(jnp.int32) * jnp.arange(node_count, dtype=jnp.int32)[None, :, None],
        axis=1,
    )
    valid = jnp.any(slot_match, axis=1)
    my_tasks = lax.dynamic_index_in_dim(task_table, own_column, 0, False)
    my_valid = lax.dynamic_index_in_dim(valid, own_column, 0, False)
    flipped = jnp.swapaxes(lower, 0, 1)
    gathered = lax.all_gather(flipped, "pcol", axis=2, tiled=True)
    halves = gathered[:, my_tasks] * my_valid[None, :, None, None].astype(jnp.bfloat16)
    task_lists = structure[my_tasks]
    pick = (task_lists == own_column).astype(jnp.bfloat16)
    own_half = jnp.einsum("cs,scrb->crb", pick, halves, preferred_element_type=jnp.float32).astype(
        jnp.bfloat16
    )
    own_full = lax.all_gather(own_half, "prow", axis=1, tiled=True)
    contribs = []
    for index_slot in range(cap_slots):
        chosen = inverse_blocks[task_lists[index_slot]]
        products = jnp.einsum(
            "sab,bc->sac", chosen, own_full[index_slot], preferred_element_type=jnp.float32
        ).astype(jnp.bfloat16)
        contribs.append(
            jnp.einsum(
                "sba,sbc->ac", halves[:, index_slot], products, preferred_element_type=jnp.float32
            )
        )
    totals = jnp.zeros((node_count, B, B), jnp.float32)
    for index_slot in range(cap_slots):
        supernode = my_tasks[index_slot]
        current = lax.dynamic_index_in_dim(totals, supernode, 0, False)
        totals = lax.dynamic_update_index_in_dim(
            totals, current + contribs[index_slot], supernode, 0
        )
    coupling = lax.psum_scatter(totals, ("prow", "pcol"), scatter_dimension=1, tiled=True)
    return diag_inverse - coupling


MESH = pl.DeviceIdType.MESH


def fused_kernel(
    columns, cap, nodes, slots,
    tasks, own_slot, structure, places,
    inverse_hbm, lower_ref, diag_hbm,
    out_ref,
    inverse_ref, diag_ref, picked, relayed, halves, full, partial, from_core, outgoing, incoming,
    load_sem, mirror_send, mirror_recv, pick_send, pick_recv, relay_send, relay_recv,
    half_send, half_recv, core_send, core_recv, out_send, out_recv,
    *mirrored,
):
    pole = lax.axis_index("pole")
    core = lax.axis_index("prow")
    me = lax.axis_index("pcol")
    other = 1 - core
    peers = columns - 1
    mates = columns // 2 - 1
    base = (me // (mates + 1)) * (mates + 1)
    mirror = columns - 2 - me + 2 * (me % 2)

    load_inverse = pltpu.make_async_copy(inverse_hbm, inverse_ref, load_sem.at[0])
    load_diag = pltpu.make_async_copy(diag_hbm, diag_ref, load_sem.at[1])

    barrier = pltpu.get_barrier_semaphore()

    def greet(step, carry):
        peer = lax.rem(me + 1 + step, columns)
        pl.semaphore_signal(barrier, inc=1, device_id=(pole, core, peer), device_id_type=MESH)
        return carry

    lax.fori_loop(0, peers, greet, 0)
    pl.semaphore_signal(barrier, inc=1, device_id=(pole, other, me), device_id_type=MESH)
    pl.semaphore_wait(barrier, columns)

    def mate(step):
        return base + lax.rem(me - base + 1 + step, mates + 1)

    def mirror_copy(slot):
        return pltpu.make_async_remote_copy(
            src_ref=lower_ref.at[:, slot],
            dst_ref=mirrored[slot],
            send_sem=mirror_send.at[slot],
            recv_sem=mirror_recv.at[slot],
            device_id=(pole, core, mirror),
            device_id_type=MESH,
        )

    def pick_copy(index, step):
        return pltpu.make_async_remote_copy(
            src_ref=picked.at[index, step],
            dst_ref=halves.at[index, me],
            send_sem=pick_send.at[index, step],
            recv_sem=pick_recv.at[index, step],
            device_id=(pole, core, mate(step)),
            device_id_type=MESH,
        )

    def relay_copy(slot, index, step):
        return pltpu.make_async_remote_copy(
            src_ref=relayed.at[slot, index, step],
            dst_ref=halves.at[index, mirror, slot],
            send_sem=relay_send.at[slot, index, step],
            recv_sem=relay_recv.at[slot, index, step],
            device_id=(pole, core, mate(step)),
            device_id_type=MESH,
        )

    def half_copy(index):
        return pltpu.make_async_remote_copy(
            src_ref=full.at[index, core],
            dst_ref=full.at[index, core],
            send_sem=half_send.at[index],
            recv_sem=half_recv.at[index],
            device_id=(pole, other, me),
            device_id_type=MESH,
        )

    def core_copy(index):
        return pltpu.make_async_remote_copy(
            src_ref=partial.at[index, other],
            dst_ref=from_core.at[index],
            send_sem=core_send.at[index],
            recv_sem=core_recv.at[index],
            device_id=(pole, other, me),
            device_id_type=MESH,
        )

    def out_copy(index, step):
        peer = lax.rem(me + 1 + step, columns)
        return pltpu.make_async_remote_copy(
            src_ref=outgoing.at[index, peer],
            dst_ref=incoming.at[me, index],
            send_sem=out_send.at[index, step],
            recv_sem=out_recv.at[index, step],
            device_id=(pole, core, peer),
            device_id_type=MESH,
        )

    def send_own(index, carry):
        def to_mate(step, inner):
            picked[index, step] = lower_ref[tasks[mate(step) * cap + index]]
            pick_copy(index, step).start()
            return inner

        lax.fori_loop(0, mates, to_mate, 0)
        halves[index, me] = lower_ref[tasks[me * cap + index]]
        return carry

    def relay_slot(slot):
        def relay_task(index, carry):
            def to_mate(step, inner):
                relayed[slot, index, step] = mirrored[slot][tasks[mate(step) * cap + index]]
                relay_copy(slot, index, step).start()
                return inner

            lax.fori_loop(0, mates, to_mate, 0)
            halves[index, mirror, slot] = mirrored[slot][tasks[me * cap + index]]
            return carry

        lax.fori_loop(0, cap, relay_task, 0)

    for slot in range(slots):
        mirror_copy(slot).start()
    load_inverse.start()
    load_diag.start()
    lax.fori_loop(0, cap, send_own, 0)
    for slot in range(slots):
        mirror_copy(slot).wait_recv()
        relay_slot(slot)
    load_inverse.wait()
    load_diag.wait()

    def arrive(index):
        def one(step, inner):
            pick_copy(index, step).wait_recv()
            for slot in range(slots):
                relay_copy(slot, index, step).wait_recv()
            return inner

        lax.fori_loop(0, mates, one, 0)
        chosen_slot = own_slot[me * cap + index]
        mine = halves[index, :, 0]
        for slot in range(1, slots):
            mine = jnp.where(chosen_slot == slot, halves[index, :, slot], mine)
        full[index, core] = mine.reshape(full.shape[2:])
        half_copy(index).start()

    def multiply(index):
        half_copy(index).wait_recv()
        node = tasks[me * cap + index]
        factor = full[index].reshape(B, B)
        total = jnp.zeros((B, B), jnp.float32)
        for slot in range(slots):
            chosen = inverse_ref[structure[node * slots + slot]]
            products = jnp.dot(chosen, factor, preferred_element_type=jnp.float32).astype(
                jnp.bfloat16
            )
            rows = halves[index, :, slot].reshape(B // 2, B)
            total = total + lax.dot_general(
                rows, products, (((0,), (0,)), ((), ())), preferred_element_type=jnp.float32
            )
        partial[index] = total.reshape(partial.shape[1:])
        core_copy(index).start()

    def hand_out(index):
        core_copy(index).wait_recv()
        summed = (partial[index, core] + from_core[index]).astype(jnp.bfloat16)
        outgoing[index] = summed.reshape(outgoing.shape[1:])
        incoming[me, index] = outgoing[index, me]

        def one(step, inner):
            out_copy(index, step).start()
            return inner

        lax.fori_loop(0, peers, one, 0)

    def step_all(step, carry):
        @pl.when(step < cap)
        def _():
            arrive(step)

        @pl.when((step >= 1) & (step < cap + 1))
        def _():
            multiply(step - 1)

        @pl.when(step >= 2)
        def _():
            hand_out(step - 2)

        return carry

    lax.fori_loop(0, cap + 2, step_all, 0)

    def landed(index, carry):
        def one(step, inner):
            out_copy(index, step).wait_recv()
            return inner

        lax.fori_loop(0, peers, one, 0)
        return carry

    lax.fori_loop(0, cap, landed, 0)

    def finish(node, carry):
        value = jnp.zeros(out_ref.shape[1:], jnp.float32)
        for slot in range(slots):
            place = node * slots + slot
            value = value + incoming[structure[place], places[place]].astype(jnp.float32)
        out_ref[node] = diag_ref[node] - value
        return carry

    lax.fori_loop(0, nodes, finish, 0)

    def sent(index, carry):
        def one_pick(step, inner):
            pick_copy(index, step).wait_send()
            for slot in range(slots):
                relay_copy(slot, index, step).wait_send()
            return inner

        def one_out(step, inner):
            out_copy(index, step).wait_send()
            return inner

        lax.fori_loop(0, mates, one_pick, 0)
        lax.fori_loop(0, peers, one_out, 0)
        half_copy(index).wait_send()
        core_copy(index).wait_send()
        return carry

    lax.fori_loop(0, cap, sent, 0)
    for slot in range(slots):
        mirror_copy(slot).wait_send()


def per_device_fused(inverse_blocks, lower, diag_inverse, structure):
    columns = lax.axis_size("pcol")
    nodes, slots = structure.shape
    chunk = lower.shape[2]
    cap = max(2, max(nodes // 4, (slots * nodes + columns - 2) // (columns - 1)))
    node_ids = jnp.arange(nodes, dtype=jnp.int32)
    matches = structure[None] == jnp.arange(columns, dtype=jnp.int32)[:, None, None]
    present = jnp.any(matches, axis=2)
    earlier = node_ids[None, :] < node_ids[:, None]
    position = jnp.sum((present[:, None, :] & earlier[None]).astype(jnp.int32), axis=2)
    hit = present[:, None, :] & (
        position[:, None, :] == jnp.arange(cap, dtype=jnp.int32)[None, :, None]
    )
    tasks = jnp.sum(jnp.where(hit, node_ids[None, None, :], 0), axis=2)
    slot_of = jnp.sum(
        jnp.where(matches, jnp.arange(slots, dtype=jnp.int32)[None, None, :], 0), axis=2
    )
    own_slot = jnp.sum(jnp.where(hit, slot_of[:, None, :], 0), axis=2)
    places = jnp.sum(jnp.where(matches, position[:, :, None], 0), axis=0)
    smem = pl.BlockSpec(memory_space=pltpu.SMEM)
    vmem = pl.BlockSpec(memory_space=pltpu.VMEM)
    anywhere = pl.BlockSpec(memory_space=pl.ANY)
    peers = columns - 1
    mates = columns // 2 - 1
    dma = pltpu.SemaphoreType.DMA
    return pl.pallas_call(
        functools.partial(fused_kernel, columns, cap, nodes, slots),
        out_shape=jax.ShapeDtypeStruct(diag_inverse.shape, jnp.float32),
        in_specs=[smem] * 4 + [anywhere, vmem, anywhere],
        out_specs=vmem,
        scratch_shapes=[
            pltpu.VMEM(inverse_blocks.shape, jnp.bfloat16),
            pltpu.VMEM(diag_inverse.shape, jnp.float32),
            pltpu.VMEM((cap, mates, slots, chunk, B), jnp.bfloat16),
            pltpu.VMEM((slots, cap, mates, chunk, B), jnp.bfloat16),
            pltpu.VMEM((cap, columns, slots, chunk, B), jnp.bfloat16),
            pltpu.VMEM((cap, 2, B // 2, B), jnp.bfloat16),
            pltpu.VMEM((cap, 2, B // 2, B), jnp.float32),
            pltpu.VMEM((cap, B // 2, B), jnp.float32),
            pltpu.VMEM((cap, columns, chunk, B), jnp.bfloat16),
            pltpu.VMEM((columns, cap, chunk, B), jnp.bfloat16),
            dma((2,)),
            dma((slots,)),
            dma((slots,)),
            dma((cap, mates)),
            dma((cap, mates)),
            dma((slots, cap, mates)),
            dma((slots, cap, mates)),
            dma((cap,)),
            dma((cap,)),
            dma((cap,)),
            dma((cap,)),
            dma((cap, peers)),
            dma((cap, peers)),
        ]
        + [pltpu.VMEM((nodes, chunk, B), jnp.bfloat16)] * slots,
        compiler_params=pltpu.CompilerParams(
            collective_id=0, has_side_effects=True, vmem_limit_bytes=48 * 1024 * 1024
        ),
    )(
        tasks.reshape(-1), own_slot.reshape(-1), structure.reshape(-1), places.reshape(-1),
        inverse_blocks, lower, diag_inverse,
    )


def solution(mesh):
    placed = (
        P("pole", "prow", "pcol"),
        P("pole", None, ("prow", "pcol"), None),
        P("pole", ("prow", "pcol"), None),
        P("pole", None),
    )
    body = per_device
    whole_tiles = B % (16 * mesh.shape["prow"] * mesh.shape["pcol"]) == 0
    if mesh.shape["prow"] == 2 and mesh.shape["pcol"] == 8 and whole_tiles:
        body = per_device_fused
    return jax.shard_map(
        body,
        mesh=mesh,
        in_specs=placed,
        out_specs=P("pole", ("prow", "pcol"), None),
        check_vma=False,
    )
```

```python
import functools

import jax
import jax.numpy as jnp
from jax import lax
from jax.experimental import pallas as pl
from jax.experimental.pallas import tpu as pltpu
from jax.sharding import PartitionSpec as P

B = 512


def per_device(inverse_blocks, lower, diag_inverse, structure):
    columns = lax.axis_size("pcol")
    own_column = lax.axis_index("pcol")
    node_count = structure.shape[0]
    slots_each = structure.shape[1]
    cap_slots = max(
        2, max(node_count // 4, (slots_each * node_count + columns - 2) // (columns - 1))
    )
    matches = structure[None, :, :] == jnp.arange(columns, dtype=jnp.int32)[:, None, None]
    present = jnp.any(matches, axis=2)
    position = jnp.cumsum(present.astype(jnp.int32), axis=1) - 1
    slot_match = present[:, :, None] & (
        position[:, :, None] == jnp.arange(cap_slots, dtype=jnp.int32)[None, None, :]
    )
    task_table = jnp.sum(
        slot_match.astype(jnp.int32) * jnp.arange(node_count, dtype=jnp.int32)[None, :, None],
        axis=1,
    )
    valid = jnp.any(slot_match, axis=1)
    my_tasks = lax.dynamic_index_in_dim(task_table, own_column, 0, False)
    my_valid = lax.dynamic_index_in_dim(valid, own_column, 0, False)
    flipped = jnp.swapaxes(lower, 0, 1)
    gathered = lax.all_gather(flipped, "pcol", axis=2, tiled=True)
    halves = gathered[:, my_tasks] * my_valid[None, :, None, None].astype(jnp.bfloat16)
    task_lists = structure[my_tasks]
    pick = (task_lists == own_column).astype(jnp.bfloat16)
    own_half = jnp.einsum("cs,scrb->crb", pick, halves, preferred_element_type=jnp.float32).astype(
        jnp.bfloat16
    )
    own_full = lax.all_gather(own_half, "prow", axis=1, tiled=True)
    contribs = []
    for index_slot in range(cap_slots):
        chosen = inverse_blocks[task_lists[index_slot]]
        products = jnp.einsum(
            "sab,bc->sac", chosen, own_full[index_slot], preferred_element_type=jnp.float32
        ).astype(jnp.bfloat16)
        contribs.append(
            jnp.einsum(
                "sba,sbc->ac", halves[:, index_slot], products, preferred_element_type=jnp.float32
            )
        )
    totals = jnp.zeros((node_count, B, B), jnp.float32)
    for index_slot in range(cap_slots):
        supernode = my_tasks[index_slot]
        current = lax.dynamic_index_in_dim(totals, supernode, 0, False)
        totals = lax.dynamic_update_index_in_dim(
            totals, current + contribs[index_slot], supernode, 0
        )
    coupling = lax.psum_scatter(totals, ("prow", "pcol"), scatter_dimension=1, tiled=True)
    return diag_inverse - coupling


MESH = pl.DeviceIdType.MESH


def fused_kernel(
    columns, cap, nodes, slots,
    tasks, own_slot, structure, places,
    inverse_hbm, lower_ref, diag_hbm,
    out_ref,
    inverse_ref, diag_ref, mirrored, picked, halves, full, partial, from_core, outgoing, incoming,
    load_sem, mirror_send, mirror_recv, pick_send, pick_recv, half_send, half_recv, core_send, core_recv, out_send, out_recv,
):
    pole = lax.axis_index("pole")
    core = lax.axis_index("prow")
    me = lax.axis_index("pcol")
    other = 1 - core
    peers = columns - 1
    mates = columns // 2 - 1
    base = (me // (mates + 1)) * (mates + 1)
    mirror = columns - 2 - me + 2 * (me % 2)
    parts = mirror_send.shape[0]
    span = nodes // parts

    load_inverse = pltpu.make_async_copy(inverse_hbm, inverse_ref, load_sem.at[0])
    load_diag = pltpu.make_async_copy(diag_hbm, diag_ref, load_sem.at[1])

    barrier = pltpu.get_barrier_semaphore()

    def greet(step, carry):
        peer = lax.rem(me + 1 + step, columns)
        pl.semaphore_signal(barrier, inc=1, device_id=(pole, core, peer), device_id_type=MESH)
        return carry

    lax.fori_loop(0, peers, greet, 0)
    pl.semaphore_signal(barrier, inc=1, device_id=(pole, other, me), device_id_type=MESH)
    pl.semaphore_wait(barrier, columns)

    def mate(step):
        return base + lax.rem(me - base + 1 + step, mates + 1)

    def mirror_copy(part):
        piece = pl.ds(part * span, span)
        return pltpu.make_async_remote_copy(
            src_ref=lower_ref.at[piece],
            dst_ref=mirrored.at[piece],
            send_sem=mirror_send.at[part],
            recv_sem=mirror_recv.at[part],
            device_id=(pole, core, mirror),
            device_id_type=MESH,
        )

    def pick_copy(relayed, index, step):
        return pltpu.make_async_remote_copy(
            src_ref=picked.at[relayed, index, step],
            dst_ref=halves.at[index, mirror if relayed else me],
            send_sem=pick_send.at[relayed, index, step],
            recv_sem=pick_recv.at[relayed, index, step],
            device_id=(pole, core, mate(step)),
            device_id_type=MESH,
        )

    def half_copy(index):
        return pltpu.make_async_remote_copy(
            src_ref=full.at[index, core],
            dst_ref=full.at[index, core],
            send_sem=half_send.at[index],
            recv_sem=half_recv.at[index],
            device_id=(pole, other, me),
            device_id_type=MESH,
        )

    def core_copy(index):
        return pltpu.make_async_remote_copy(
            src_ref=partial.at[index, other],
            dst_ref=from_core.at[index],
            send_sem=core_send.at[index],
            recv_sem=core_recv.at[index],
            device_id=(pole, other, me),
            device_id_type=MESH,
        )

    def out_copy(index, step):
        peer = lax.rem(me + 1 + step, columns)
        return pltpu.make_async_remote_copy(
            src_ref=outgoing.at[index, peer],
            dst_ref=incoming.at[me, index],
            send_sem=out_send.at[index, step],
            recv_sem=out_recv.at[index, step],
            device_id=(pole, core, peer),
            device_id_type=MESH,
        )

    def send_tasks(relayed, source):
        def send_task(index, carry):
            def to_mate(step, inner):
                picked[relayed, index, step] = source[tasks[mate(step) * cap + index]]
                pick_copy(relayed, index, step).start()
                return inner

            lax.fori_loop(0, mates, to_mate, 0)
            halves[index, mirror if relayed else me] = source[tasks[me * cap + index]]
            return carry

        lax.fori_loop(0, cap, send_task, 0)

    for part in range(parts):
        mirror_copy(part).start()
    load_inverse.start()
    load_diag.start()
    send_tasks(0, lower_ref)
    for part in range(parts):
        mirror_copy(part).wait_recv()
    send_tasks(1, mirrored)
    load_inverse.wait()
    load_diag.wait()

    def arrive(index):
        def one(step, inner):
            pick_copy(0, index, step).wait_recv()
            pick_copy(1, index, step).wait_recv()
            return inner

        lax.fori_loop(0, mates, one, 0)
        chosen_slot = own_slot[me * cap + index]
        mine = halves[index, :, 0]
        for slot in range(1, slots):
            mine = jnp.where(chosen_slot == slot, halves[index, :, slot], mine)
        full[index, core] = mine.reshape(full.shape[2:])
        half_copy(index).start()

    def multiply(index):
        half_copy(index).wait_recv()
        node = tasks[me * cap + index]
        factor = full[index].reshape(B, B)
        chosen = jnp.concatenate(
            [inverse_ref[structure[node * slots + slot]] for slot in range(slots)], axis=0
        )
        products = jnp.dot(chosen, factor, preferred_element_type=jnp.float32).astype(
            jnp.bfloat16
        )
        rows = jnp.concatenate(
            [halves[index, :, slot].reshape(B // 2, B) for slot in range(slots)], axis=0
        )
        total = lax.dot_general(
            rows, products, (((0,), (0,)), ((), ())), preferred_element_type=jnp.float32
        )
        partial[index] = total.reshape(partial.shape[1:])
        core_copy(index).start()

    def hand_out(index):
        core_copy(index).wait_recv()
        summed = (partial[index, core] + from_core[index]).astype(jnp.bfloat16)
        outgoing[index] = summed.reshape(outgoing.shape[1:])
        incoming[me, index] = outgoing[index, me]

        def one(step, inner):
            out_copy(index, step).start()
            return inner

        lax.fori_loop(0, peers, one, 0)

    def step_all(step, carry):
        @pl.when(step < cap)
        def _():
            arrive(step)

        @pl.when((step >= 1) & (step < cap + 1))
        def _():
            multiply(step - 1)

        @pl.when(step >= 2)
        def _():
            hand_out(step - 2)

        return carry

    lax.fori_loop(0, cap + 2, step_all, 0)

    def landed(index, carry):
        def one(step, inner):
            out_copy(index, step).wait_recv()
            return inner

        lax.fori_loop(0, peers, one, 0)
        return carry

    lax.fori_loop(0, cap, landed, 0)

    def finish(node, carry):
        value = jnp.zeros(out_ref.shape[1:], jnp.float32)
        for slot in range(slots):
            place = node * slots + slot
            value = value + incoming[structure[place], places[place]].astype(jnp.float32)
        out_ref[node] = diag_ref[node] - value
        return carry

    lax.fori_loop(0, nodes, finish, 0)

    def sent(index, carry):
        def one_pick(step, inner):
            pick_copy(0, index, step).wait_send()
            pick_copy(1, index, step).wait_send()
            return inner

        def one_out(step, inner):
            out_copy(index, step).wait_send()
            return inner

        lax.fori_loop(0, mates, one_pick, 0)
        lax.fori_loop(0, peers, one_out, 0)
        half_copy(index).wait_send()
        core_copy(index).wait_send()
        return carry

    lax.fori_loop(0, cap, sent, 0)
    for part in range(parts):
        mirror_copy(part).wait_send()


def per_device_fused(inverse_blocks, lower, diag_inverse, structure):
    columns = lax.axis_size("pcol")
    nodes, slots = structure.shape
    chunk = lower.shape[2]
    cap = max(2, max(nodes // 4, (slots * nodes + columns - 2) // (columns - 1)))
    node_ids = jnp.arange(nodes, dtype=jnp.int32)
    matches = structure[None] == jnp.arange(columns, dtype=jnp.int32)[:, None, None]
    present = jnp.any(matches, axis=2)
    earlier = node_ids[None, :] < node_ids[:, None]
    position = jnp.sum((present[:, None, :] & earlier[None]).astype(jnp.int32), axis=2)
    hit = present[:, None, :] & (
        position[:, None, :] == jnp.arange(cap, dtype=jnp.int32)[None, :, None]
    )
    tasks = jnp.sum(jnp.where(hit, node_ids[None, None, :], 0), axis=2)
    slot_of = jnp.sum(
        jnp.where(matches, jnp.arange(slots, dtype=jnp.int32)[None, None, :], 0), axis=2
    )
    own_slot = jnp.sum(jnp.where(hit, slot_of[:, None, :], 0), axis=2)
    places = jnp.sum(jnp.where(matches, position[:, :, None], 0), axis=0)
    smem = pl.BlockSpec(memory_space=pltpu.SMEM)
    vmem = pl.BlockSpec(memory_space=pltpu.VMEM)
    anywhere = pl.BlockSpec(memory_space=pl.ANY)
    peers = columns - 1
    mates = columns // 2 - 1
    parts = 4 if nodes % 4 == 0 else 1
    dma = pltpu.SemaphoreType.DMA
    return pl.pallas_call(
        functools.partial(fused_kernel, columns, cap, nodes, slots),
        out_shape=jax.ShapeDtypeStruct(diag_inverse.shape, jnp.float32),
        in_specs=[smem] * 4 + [anywhere, vmem, anywhere],
        out_specs=vmem,
        scratch_shapes=[
            pltpu.VMEM(inverse_blocks.shape, jnp.bfloat16),
            pltpu.VMEM(diag_inverse.shape, jnp.float32),
            pltpu.VMEM(lower.shape, jnp.bfloat16),
            pltpu.VMEM((2, cap, mates, slots, chunk, B), jnp.bfloat16),
            pltpu.VMEM((cap, columns, slots, chunk, B), jnp.bfloat16),
            pltpu.VMEM((cap, 2, B // 2, B), jnp.bfloat16),
            pltpu.VMEM((cap, 2, B // 2, B), jnp.float32),
            pltpu.VMEM((cap, B // 2, B), jnp.float32),
            pltpu.VMEM((cap, columns, chunk, B), jnp.bfloat16),
            pltpu.VMEM((columns, cap, chunk, B), jnp.bfloat16),
            dma((2,)),
            dma((parts,)),
            dma((parts,)),
            dma((2, cap, mates)),
            dma((2, cap, mates)),
            dma((cap,)),
            dma((cap,)),
            dma((cap,)),
            dma((cap,)),
            dma((cap, peers)),
            dma((cap, peers)),
        ],
        compiler_params=pltpu.CompilerParams(
            collective_id=0, has_side_effects=True, vmem_limit_bytes=48 * 1024 * 1024
        ),
    )(
        tasks.reshape(-1), own_slot.reshape(-1), structure.reshape(-1), places.reshape(-1),
        inverse_blocks, lower, diag_inverse,
    )


def solution(mesh):
    placed = (
        P("pole", "prow", "pcol"),
        P("pole", None, ("prow", "pcol"), None),
        P("pole", ("prow", "pcol"), None),
        P("pole", None),
    )
    body = per_device
    whole_tiles = B % (16 * mesh.shape["prow"] * mesh.shape["pcol"]) == 0
    if mesh.shape["prow"] == 2 and mesh.shape["pcol"] == 8 and whole_tiles:
        body = per_device_fused
    return jax.shard_map(
        body,
        mesh=mesh,
        in_specs=placed,
        out_specs=P("pole", ("prow", "pcol"), None),
        check_vma=False,
    )
```

```python
import functools

import jax
import jax.numpy as jnp
from jax import lax
from jax.experimental import pallas as pl
from jax.experimental.pallas import tpu as pltpu
from jax.sharding import PartitionSpec as P

B = 512


def per_device(inverse_blocks, lower, diag_inverse, structure):
    columns = lax.axis_size("pcol")
    own_column = lax.axis_index("pcol")
    node_count = structure.shape[0]
    slots_each = structure.shape[1]
    cap_slots = max(
        2, max(node_count // 4, (slots_each * node_count + columns - 2) // (columns - 1))
    )
    matches = structure[None, :, :] == jnp.arange(columns, dtype=jnp.int32)[:, None, None]
    present = jnp.any(matches, axis=2)
    position = jnp.cumsum(present.astype(jnp.int32), axis=1) - 1
    slot_match = present[:, :, None] & (
        position[:, :, None] == jnp.arange(cap_slots, dtype=jnp.int32)[None, None, :]
    )
    task_table = jnp.sum(
        slot_match.astype(jnp.int32) * jnp.arange(node_count, dtype=jnp.int32)[None, :, None],
        axis=1,
    )
    valid = jnp.any(slot_match, axis=1)
    my_tasks = lax.dynamic_index_in_dim(task_table, own_column, 0, False)
    my_valid = lax.dynamic_index_in_dim(valid, own_column, 0, False)
    flipped = jnp.swapaxes(lower, 0, 1)
    gathered = lax.all_gather(flipped, "pcol", axis=2, tiled=True)
    halves = gathered[:, my_tasks] * my_valid[None, :, None, None].astype(jnp.bfloat16)
    task_lists = structure[my_tasks]
    pick = (task_lists == own_column).astype(jnp.bfloat16)
    own_half = jnp.einsum("cs,scrb->crb", pick, halves, preferred_element_type=jnp.float32).astype(
        jnp.bfloat16
    )
    own_full = lax.all_gather(own_half, "prow", axis=1, tiled=True)
    contribs = []
    for index_slot in range(cap_slots):
        chosen = inverse_blocks[task_lists[index_slot]]
        products = jnp.einsum(
            "sab,bc->sac", chosen, own_full[index_slot], preferred_element_type=jnp.float32
        ).astype(jnp.bfloat16)
        contribs.append(
            jnp.einsum(
                "sba,sbc->ac", halves[:, index_slot], products, preferred_element_type=jnp.float32
            )
        )
    totals = jnp.zeros((node_count, B, B), jnp.float32)
    for index_slot in range(cap_slots):
        supernode = my_tasks[index_slot]
        current = lax.dynamic_index_in_dim(totals, supernode, 0, False)
        totals = lax.dynamic_update_index_in_dim(
            totals, current + contribs[index_slot], supernode, 0
        )
    coupling = lax.psum_scatter(totals, ("prow", "pcol"), scatter_dimension=1, tiled=True)
    return diag_inverse - coupling


MESH = pl.DeviceIdType.MESH


def fused_kernel(
    columns, cap, nodes, slots,
    tasks, own_slot, structure, places,
    inverse_hbm, lower_ref, diag_hbm,
    out_ref,
    inverse_ref, diag_ref, mirrored, picked, halves, full, partial, from_core, outgoing, incoming,
    load_sem, mirror_send, mirror_recv, pick_send, pick_recv, half_send, half_recv, core_send, core_recv, out_send, out_recv,
):
    pole = lax.axis_index("pole")
    core = lax.axis_index("prow")
    me = lax.axis_index("pcol")
    other = 1 - core
    peers = columns - 1
    mates = columns // 2 - 1
    ahead = min(4, cap)
    base = (me // (mates + 1)) * (mates + 1)
    mirror = columns - 2 - me + 2 * (me % 2)
    parts = mirror_send.shape[0]
    span = nodes // parts

    load_inverse = pltpu.make_async_copy(inverse_hbm, inverse_ref, load_sem.at[0])
    load_diag = pltpu.make_async_copy(diag_hbm, diag_ref, load_sem.at[1])

    barrier = pltpu.get_barrier_semaphore()

    def greet(step, carry):
        peer = lax.rem(me + 1 + step, columns)
        pl.semaphore_signal(barrier, inc=1, device_id=(pole, core, peer), device_id_type=MESH)
        return carry

    lax.fori_loop(0, peers, greet, 0)
    pl.semaphore_signal(barrier, inc=1, device_id=(pole, other, me), device_id_type=MESH)
    pl.semaphore_wait(barrier, columns)

    def mate(step):
        return base + lax.rem(me - base + 1 + step, mates + 1)

    def mirror_copy(part):
        piece = pl.ds(part * span, span)
        return pltpu.make_async_remote_copy(
            src_ref=lower_ref.at[piece],
            dst_ref=mirrored.at[piece],
            send_sem=mirror_send.at[part],
            recv_sem=mirror_recv.at[part],
            device_id=(pole, core, mirror),
            device_id_type=MESH,
        )

    def pick_copy(relayed, index, step):
        return pltpu.make_async_remote_copy(
            src_ref=picked.at[relayed, index, step],
            dst_ref=halves.at[index, mirror if relayed else me],
            send_sem=pick_send.at[relayed, index, step],
            recv_sem=pick_recv.at[relayed, index, step],
            device_id=(pole, core, mate(step)),
            device_id_type=MESH,
        )

    def half_copy(index):
        return pltpu.make_async_remote_copy(
            src_ref=full.at[index, core],
            dst_ref=full.at[index, core],
            send_sem=half_send.at[index],
            recv_sem=half_recv.at[index],
            device_id=(pole, other, me),
            device_id_type=MESH,
        )

    def core_copy(index):
        return pltpu.make_async_remote_copy(
            src_ref=partial.at[index, other],
            dst_ref=from_core.at[index],
            send_sem=core_send.at[index],
            recv_sem=core_recv.at[index],
            device_id=(pole, other, me),
            device_id_type=MESH,
        )

    def out_copy(index, step):
        peer = lax.rem(me + 1 + step, columns)
        return pltpu.make_async_remote_copy(
            src_ref=outgoing.at[index, peer],
            dst_ref=incoming.at[me, index],
            send_sem=out_send.at[index, step],
            recv_sem=out_recv.at[index, step],
            device_id=(pole, core, peer),
            device_id_type=MESH,
        )

    def send_task(relayed, source, index):
        def to_mate(step, inner):
            picked[relayed, index, step] = source[tasks[mate(step) * cap + index]]
            pick_copy(relayed, index, step).start()
            return inner

        lax.fori_loop(0, mates, to_mate, 0)
        halves[index, mirror if relayed else me] = source[tasks[me * cap + index]]

    def send_own(index, carry):
        send_task(0, lower_ref, index)
        return carry

    for part in range(parts):
        mirror_copy(part).start()
    load_inverse.start()
    load_diag.start()
    lax.fori_loop(0, cap, send_own, 0)
    for part in range(parts):
        mirror_copy(part).wait_recv()
    for index in range(ahead):
        send_task(1, mirrored, index)
    load_inverse.wait()
    load_diag.wait()

    def arrive(index):
        def one(step, inner):
            pick_copy(0, index, step).wait_recv()
            pick_copy(1, index, step).wait_recv()
            return inner

        lax.fori_loop(0, mates, one, 0)
        chosen_slot = own_slot[me * cap + index]
        mine = halves[index, :, 0]
        for slot in range(1, slots):
            mine = jnp.where(chosen_slot == slot, halves[index, :, slot], mine)
        full[index, core] = mine.reshape(full.shape[2:])
        half_copy(index).start()

    def multiply(index):
        half_copy(index).wait_recv()
        node = tasks[me * cap + index]
        factor = full[index].reshape(B, B)
        chosen = jnp.concatenate(
            [inverse_ref[structure[node * slots + slot]] for slot in range(slots)], axis=0
        )
        products = jnp.dot(chosen, factor, preferred_element_type=jnp.float32).astype(
            jnp.bfloat16
        )
        rows = jnp.concatenate(
            [halves[index, :, slot].reshape(B // 2, B) for slot in range(slots)], axis=0
        )
        total = lax.dot_general(
            rows, products, (((0,), (0,)), ((), ())), preferred_element_type=jnp.float32
        )
        partial[index] = total.reshape(partial.shape[1:])
        core_copy(index).start()

    def hand_out(index):
        core_copy(index).wait_recv()
        summed = (partial[index, core] + from_core[index]).astype(jnp.bfloat16)
        outgoing[index] = summed.reshape(outgoing.shape[1:])
        incoming[me, index] = outgoing[index, me]

        def one(step, inner):
            out_copy(index, step).start()
            return inner

        lax.fori_loop(0, peers, one, 0)

    def step_all(step, carry):
        @pl.when(step < cap)
        def _():
            arrive(step)

        @pl.when(step < cap - ahead)
        def _():
            send_task(1, mirrored, step + ahead)

        @pl.when((step >= 1) & (step < cap + 1))
        def _():
            multiply(step - 1)

        @pl.when(step >= 2)
        def _():
            hand_out(step - 2)

        return carry

    lax.fori_loop(0, cap + 2, step_all, 0)

    def landed(index, carry):
        def one(step, inner):
            out_copy(index, step).wait_recv()
            return inner

        lax.fori_loop(0, peers, one, 0)
        return carry

    lax.fori_loop(0, cap, landed, 0)

    def finish(node, carry):
        value = jnp.zeros(out_ref.shape[1:], jnp.float32)
        for slot in range(slots):
            place = node * slots + slot
            value = value + incoming[structure[place], places[place]].astype(jnp.float32)
        out_ref[node] = diag_ref[node] - value
        return carry

    lax.fori_loop(0, nodes, finish, 0)

    def sent(index, carry):
        def one_pick(step, inner):
            pick_copy(0, index, step).wait_send()
            pick_copy(1, index, step).wait_send()
            return inner

        def one_out(step, inner):
            out_copy(index, step).wait_send()
            return inner

        lax.fori_loop(0, mates, one_pick, 0)
        lax.fori_loop(0, peers, one_out, 0)
        half_copy(index).wait_send()
        core_copy(index).wait_send()
        return carry

    lax.fori_loop(0, cap, sent, 0)
    for part in range(parts):
        mirror_copy(part).wait_send()


def per_device_fused(inverse_blocks, lower, diag_inverse, structure):
    columns = lax.axis_size("pcol")
    nodes, slots = structure.shape
    chunk = lower.shape[2]
    cap = max(2, max(nodes // 4, (slots * nodes + columns - 2) // (columns - 1)))
    node_ids = jnp.arange(nodes, dtype=jnp.int32)
    matches = structure[None] == jnp.arange(columns, dtype=jnp.int32)[:, None, None]
    present = jnp.any(matches, axis=2)
    earlier = node_ids[None, :] < node_ids[:, None]
    position = jnp.sum((present[:, None, :] & earlier[None]).astype(jnp.int32), axis=2)
    hit = present[:, None, :] & (
        position[:, None, :] == jnp.arange(cap, dtype=jnp.int32)[None, :, None]
    )
    tasks = jnp.sum(jnp.where(hit, node_ids[None, None, :], 0), axis=2)
    slot_of = jnp.sum(
        jnp.where(matches, jnp.arange(slots, dtype=jnp.int32)[None, None, :], 0), axis=2
    )
    own_slot = jnp.sum(jnp.where(hit, slot_of[:, None, :], 0), axis=2)
    places = jnp.sum(jnp.where(matches, position[:, :, None], 0), axis=0)
    smem = pl.BlockSpec(memory_space=pltpu.SMEM)
    vmem = pl.BlockSpec(memory_space=pltpu.VMEM)
    anywhere = pl.BlockSpec(memory_space=pl.ANY)
    peers = columns - 1
    mates = columns // 2 - 1
    parts = 4 if nodes % 4 == 0 else 1
    dma = pltpu.SemaphoreType.DMA
    return pl.pallas_call(
        functools.partial(fused_kernel, columns, cap, nodes, slots),
        out_shape=jax.ShapeDtypeStruct(diag_inverse.shape, jnp.float32),
        in_specs=[smem] * 4 + [anywhere, vmem, anywhere],
        out_specs=vmem,
        scratch_shapes=[
            pltpu.VMEM(inverse_blocks.shape, jnp.bfloat16),
            pltpu.VMEM(diag_inverse.shape, jnp.float32),
            pltpu.VMEM(lower.shape, jnp.bfloat16),
            pltpu.VMEM((2, cap, mates, slots, chunk, B), jnp.bfloat16),
            pltpu.VMEM((cap, columns, slots, chunk, B), jnp.bfloat16),
            pltpu.VMEM((cap, 2, B // 2, B), jnp.bfloat16),
            pltpu.VMEM((cap, 2, B // 2, B), jnp.float32),
            pltpu.VMEM((cap, B // 2, B), jnp.float32),
            pltpu.VMEM((cap, columns, chunk, B), jnp.bfloat16),
            pltpu.VMEM((columns, cap, chunk, B), jnp.bfloat16),
            dma((2,)),
            dma((parts,)),
            dma((parts,)),
            dma((2, cap, mates)),
            dma((2, cap, mates)),
            dma((cap,)),
            dma((cap,)),
            dma((cap,)),
            dma((cap,)),
            dma((cap, peers)),
            dma((cap, peers)),
        ],
        compiler_params=pltpu.CompilerParams(
            collective_id=0, has_side_effects=True, vmem_limit_bytes=48 * 1024 * 1024
        ),
    )(
        tasks.reshape(-1), own_slot.reshape(-1), structure.reshape(-1), places.reshape(-1),
        inverse_blocks, lower, diag_inverse,
    )


def solution(mesh):
    placed = (
        P("pole", "prow", "pcol"),
        P("pole", None, ("prow", "pcol"), None),
        P("pole", ("prow", "pcol"), None),
        P("pole", None),
    )
    body = per_device
    whole_tiles = B % (16 * mesh.shape["prow"] * mesh.shape["pcol"]) == 0
    if mesh.shape["prow"] == 2 and mesh.shape["pcol"] == 8 and whole_tiles:
        body = per_device_fused
    return jax.shard_map(
        body,
        mesh=mesh,
        in_specs=placed,
        out_specs=P("pole", ("prow", "pcol"), None),
        check_vma=False,
    )
```

```python
import functools

import jax
import jax.numpy as jnp
from jax import lax
from jax.experimental import pallas as pl
from jax.experimental.pallas import tpu as pltpu
from jax.sharding import PartitionSpec as P

B = 512


def per_device(inverse_blocks, lower, diag_inverse, structure):
    columns = lax.axis_size("pcol")
    own_column = lax.axis_index("pcol")
    node_count = structure.shape[0]
    slots_each = structure.shape[1]
    cap_slots = max(
        2, max(node_count // 4, (slots_each * node_count + columns - 2) // (columns - 1))
    )
    matches = structure[None, :, :] == jnp.arange(columns, dtype=jnp.int32)[:, None, None]
    present = jnp.any(matches, axis=2)
    position = jnp.cumsum(present.astype(jnp.int32), axis=1) - 1
    slot_match = present[:, :, None] & (
        position[:, :, None] == jnp.arange(cap_slots, dtype=jnp.int32)[None, None, :]
    )
    task_table = jnp.sum(
        slot_match.astype(jnp.int32) * jnp.arange(node_count, dtype=jnp.int32)[None, :, None],
        axis=1,
    )
    valid = jnp.any(slot_match, axis=1)
    my_tasks = lax.dynamic_index_in_dim(task_table, own_column, 0, False)
    my_valid = lax.dynamic_index_in_dim(valid, own_column, 0, False)
    flipped = jnp.swapaxes(lower, 0, 1)
    gathered = lax.all_gather(flipped, "pcol", axis=2, tiled=True)
    halves = gathered[:, my_tasks] * my_valid[None, :, None, None].astype(jnp.bfloat16)
    task_lists = structure[my_tasks]
    pick = (task_lists == own_column).astype(jnp.bfloat16)
    own_half = jnp.einsum("cs,scrb->crb", pick, halves, preferred_element_type=jnp.float32).astype(
        jnp.bfloat16
    )
    own_full = lax.all_gather(own_half, "prow", axis=1, tiled=True)
    contribs = []
    for index_slot in range(cap_slots):
        chosen = inverse_blocks[task_lists[index_slot]]
        products = jnp.einsum(
            "sab,bc->sac", chosen, own_full[index_slot], preferred_element_type=jnp.float32
        ).astype(jnp.bfloat16)
        contribs.append(
            jnp.einsum(
                "sba,sbc->ac", halves[:, index_slot], products, preferred_element_type=jnp.float32
            )
        )
    totals = jnp.zeros((node_count, B, B), jnp.float32)
    for index_slot in range(cap_slots):
        supernode = my_tasks[index_slot]
        current = lax.dynamic_index_in_dim(totals, supernode, 0, False)
        totals = lax.dynamic_update_index_in_dim(
            totals, current + contribs[index_slot], supernode, 0
        )
    coupling = lax.psum_scatter(totals, ("prow", "pcol"), scatter_dimension=1, tiled=True)
    return diag_inverse - coupling


MESH = pl.DeviceIdType.MESH


def fused_kernel(
    columns, cap, nodes, slots,
    tasks, own_slot, structure, places,
    inverse_hbm, lower_ref, diag_hbm,
    out_ref,
    inverse_ref, diag_ref, mirrored, picked, halves, full, partial, from_core, outgoing, incoming,
    load_sem, mirror_send, mirror_recv, pick_send, pick_recv, half_send, half_recv, core_send, core_recv, out_send, out_recv,
):
    pole = lax.axis_index("pole")
    core = lax.axis_index("prow")
    me = lax.axis_index("pcol")
    other = 1 - core
    peers = columns - 1
    mates = columns // 2 - 1
    base = (me // (mates + 1)) * (mates + 1)
    mirror = columns - 2 - me + 2 * (me % 2)
    parts = mirror_send.shape[0]
    span = nodes // parts

    load_inverse = pltpu.make_async_copy(inverse_hbm, inverse_ref, load_sem.at[0])
    load_diag = pltpu.make_async_copy(diag_hbm, diag_ref, load_sem.at[1])

    barrier = pltpu.get_barrier_semaphore()

    def greet(step, carry):
        peer = lax.rem(me + 1 + step, columns)
        pl.semaphore_signal(barrier, inc=1, device_id=(pole, core, peer), device_id_type=MESH)
        return carry

    lax.fori_loop(0, peers, greet, 0)
    pl.semaphore_signal(barrier, inc=1, device_id=(pole, other, me), device_id_type=MESH)
    pl.semaphore_wait(barrier, columns)

    def mate(step):
        return base + lax.rem(me - base + 1 + step, mates + 1)

    def mirror_copy(part):
        piece = pl.ds(part * span, span)
        return pltpu.make_async_remote_copy(
            src_ref=lower_ref.at[piece],
            dst_ref=mirrored.at[piece],
            send_sem=mirror_send.at[part],
            recv_sem=mirror_recv.at[part],
            device_id=(pole, core, mirror),
            device_id_type=MESH,
        )

    def pick_copy(relayed, index, step):
        return pltpu.make_async_remote_copy(
            src_ref=picked.at[relayed, index, step],
            dst_ref=halves.at[index, mirror if relayed else me],
            send_sem=pick_send.at[relayed, index, step],
            recv_sem=pick_recv.at[relayed, index, step],
            device_id=(pole, core, mate(step)),
            device_id_type=MESH,
        )

    def half_copy(index):
        return pltpu.make_async_remote_copy(
            src_ref=full.at[index, core],
            dst_ref=full.at[index, core],
            send_sem=half_send.at[index],
            recv_sem=half_recv.at[index],
            device_id=(pole, other, me),
            device_id_type=MESH,
        )

    def core_copy(index):
        return pltpu.make_async_remote_copy(
            src_ref=partial.at[index, other],
            dst_ref=from_core.at[index],
            send_sem=core_send.at[index],
            recv_sem=core_recv.at[index],
            device_id=(pole, other, me),
            device_id_type=MESH,
        )

    def out_copy(index, step):
        peer = lax.rem(me + 1 + lax.rem(step + columns // 2 - 1, peers), columns)
        return pltpu.make_async_remote_copy(
            src_ref=outgoing.at[index, peer],
            dst_ref=incoming.at[me, index],
            send_sem=out_send.at[index, step],
            recv_sem=out_recv.at[index, step],
            device_id=(pole, core, peer),
            device_id_type=MESH,
        )

    def send_tasks(relayed, source):
        def send_task(index, carry):
            def to_mate(step, inner):
                picked[relayed, index, step] = source[tasks[mate(step) * cap + index]]
                pick_copy(relayed, index, step).start()
                return inner

            lax.fori_loop(0, mates, to_mate, 0)
            halves[index, mirror if relayed else me] = source[tasks[me * cap + index]]
            return carry

        lax.fori_loop(0, cap, send_task, 0)

    for part in range(parts):
        mirror_copy(part).start()
    load_inverse.start()
    load_diag.start()
    send_tasks(0, lower_ref)
    for part in range(parts):
        mirror_copy(part).wait_recv()
    send_tasks(1, mirrored)
    load_inverse.wait()
    load_diag.wait()

    def arrive(index):
        def one(step, inner):
            pick_copy(0, index, step).wait_recv()
            pick_copy(1, index, step).wait_recv()
            return inner

        lax.fori_loop(0, mates, one, 0)
        chosen_slot = own_slot[me * cap + index]
        mine = halves[index, :, 0]
        for slot in range(1, slots):
            mine = jnp.where(chosen_slot == slot, halves[index, :, slot], mine)
        full[index, core] = mine.reshape(full.shape[2:])
        half_copy(index).start()

    def multiply(index):
        half_copy(index).wait_recv()
        node = tasks[me * cap + index]
        factor = full[index].reshape(B, B)
        total = jnp.zeros((B, B), jnp.float32)
        for slot in range(slots):
            chosen = inverse_ref[structure[node * slots + slot]]
            products = jnp.dot(chosen, factor, preferred_element_type=jnp.float32).astype(
                jnp.bfloat16
            )
            rows = halves[index, :, slot].reshape(B // 2, B)
            total = total + lax.dot_general(
                rows, products, (((0,), (0,)), ((), ())), preferred_element_type=jnp.float32
            )
        partial[index] = total.reshape(partial.shape[1:])
        core_copy(index).start()

    def hand_out(index):
        core_copy(index).wait_recv()
        summed = (partial[index, core] + from_core[index]).astype(jnp.bfloat16)
        outgoing[index] = summed.reshape(outgoing.shape[1:])
        incoming[me, index] = outgoing[index, me]

        def one(step, inner):
            out_copy(index, step).start()
            return inner

        lax.fori_loop(0, peers, one, 0)

    def step_all(step, carry):
        @pl.when(step < cap)
        def _():
            arrive(step)

        @pl.when((step >= 1) & (step < cap + 1))
        def _():
            multiply(step - 1)

        @pl.when(step >= 2)
        def _():
            hand_out(step - 2)

        return carry

    lax.fori_loop(0, cap + 2, step_all, 0)

    def landed(index, carry):
        def one(step, inner):
            out_copy(index, step).wait_recv()
            return inner

        lax.fori_loop(0, peers, one, 0)
        return carry

    lax.fori_loop(0, cap, landed, 0)

    def finish(node, carry):
        value = jnp.zeros(out_ref.shape[1:], jnp.float32)
        for slot in range(slots):
            place = node * slots + slot
            value = value + incoming[structure[place], places[place]].astype(jnp.float32)
        out_ref[node] = diag_ref[node] - value
        return carry

    lax.fori_loop(0, nodes, finish, 0)

    def sent(index, carry):
        def one_pick(step, inner):
            pick_copy(0, index, step).wait_send()
            pick_copy(1, index, step).wait_send()
            return inner

        def one_out(step, inner):
            out_copy(index, step).wait_send()
            return inner

        lax.fori_loop(0, mates, one_pick, 0)
        lax.fori_loop(0, peers, one_out, 0)
        half_copy(index).wait_send()
        core_copy(index).wait_send()
        return carry

    lax.fori_loop(0, cap, sent, 0)
    for part in range(parts):
        mirror_copy(part).wait_send()


def per_device_fused(inverse_blocks, lower, diag_inverse, structure):
    columns = lax.axis_size("pcol")
    nodes, slots = structure.shape
    chunk = lower.shape[2]
    cap = max(2, max(nodes // 4, (slots * nodes + columns - 2) // (columns - 1)))
    node_ids = jnp.arange(nodes, dtype=jnp.int32)
    matches = structure[None] == jnp.arange(columns, dtype=jnp.int32)[:, None, None]
    present = jnp.any(matches, axis=2)
    earlier = node_ids[None, :] < node_ids[:, None]
    position = jnp.sum((present[:, None, :] & earlier[None]).astype(jnp.int32), axis=2)
    hit = present[:, None, :] & (
        position[:, None, :] == jnp.arange(cap, dtype=jnp.int32)[None, :, None]
    )
    tasks = jnp.sum(jnp.where(hit, node_ids[None, None, :], 0), axis=2)
    slot_of = jnp.sum(
        jnp.where(matches, jnp.arange(slots, dtype=jnp.int32)[None, None, :], 0), axis=2
    )
    own_slot = jnp.sum(jnp.where(hit, slot_of[:, None, :], 0), axis=2)
    places = jnp.sum(jnp.where(matches, position[:, :, None], 0), axis=0)
    smem = pl.BlockSpec(memory_space=pltpu.SMEM)
    vmem = pl.BlockSpec(memory_space=pltpu.VMEM)
    anywhere = pl.BlockSpec(memory_space=pl.ANY)
    peers = columns - 1
    mates = columns // 2 - 1
    parts = 4 if nodes % 4 == 0 else 1
    dma = pltpu.SemaphoreType.DMA
    return pl.pallas_call(
        functools.partial(fused_kernel, columns, cap, nodes, slots),
        out_shape=jax.ShapeDtypeStruct(diag_inverse.shape, jnp.float32),
        in_specs=[smem] * 4 + [anywhere, vmem, anywhere],
        out_specs=vmem,
        scratch_shapes=[
            pltpu.VMEM(inverse_blocks.shape, jnp.bfloat16),
            pltpu.VMEM(diag_inverse.shape, jnp.float32),
            pltpu.VMEM(lower.shape, jnp.bfloat16),
            pltpu.VMEM((2, cap, mates, slots, chunk, B), jnp.bfloat16),
            pltpu.VMEM((cap, columns, slots, chunk, B), jnp.bfloat16),
            pltpu.VMEM((cap, 2, B // 2, B), jnp.bfloat16),
            pltpu.VMEM((cap, 2, B // 2, B), jnp.float32),
            pltpu.VMEM((cap, B // 2, B), jnp.float32),
            pltpu.VMEM((cap, columns, chunk, B), jnp.bfloat16),
            pltpu.VMEM((columns, cap, chunk, B), jnp.bfloat16),
            dma((2,)),
            dma((parts,)),
            dma((parts,)),
            dma((2, cap, mates)),
            dma((2, cap, mates)),
            dma((cap,)),
            dma((cap,)),
            dma((cap,)),
            dma((cap,)),
            dma((cap, peers)),
            dma((cap, peers)),
        ],
        compiler_params=pltpu.CompilerParams(
            collective_id=0, has_side_effects=True, vmem_limit_bytes=48 * 1024 * 1024
        ),
    )(
        tasks.reshape(-1), own_slot.reshape(-1), structure.reshape(-1), places.reshape(-1),
        inverse_blocks, lower, diag_inverse,
    )


def solution(mesh):
    placed = (
        P("pole", "prow", "pcol"),
        P("pole", None, ("prow", "pcol"), None),
        P("pole", ("prow", "pcol"), None),
        P("pole", None),
    )
    body = per_device
    whole_tiles = B % (16 * mesh.shape["prow"] * mesh.shape["pcol"]) == 0
    if mesh.shape["prow"] == 2 and mesh.shape["pcol"] == 8 and whole_tiles:
        body = per_device_fused
    return jax.shard_map(
        body,
        mesh=mesh,
        in_specs=placed,
        out_specs=P("pole", ("prow", "pcol"), None),
        check_vma=False,
    )
```
